32 devices in a mesh: ctx: 8 (over y, x, core), head: 4 (over z).
Axes of the slice: x: 2, y: 2, z: 4, core: 2. Of those that a mesh axis runs over, the one named last changes fastest.
Arguments:
- queries: bfloat16 [2048, 2048], P('ctx', 'head'), may hold values from -120 to 120
- key_rows: bfloat16 [2048, 128], P('ctx'), may hold values from -4 to 4
- value_rows: bfloat16 [2048, 128], P('ctx'), may hold values from -6 to 6
- lengths: int32 [8], replicated, may hold values from 1 to 1024, 2048 in all
- out_weight: bfloat16 [2048, 8192], P('head'), may hold values from -0.125 to 0.125
Outputs:
- layer_out: bfloat16 [2048, 8192], P(('ctx', 'head'))
The draws below stay inside these ranges and needn't reach their ends.
Inputs may be any that keep to these rules, and one draw needn't show every extreme that they name: The lengths of the 8 documents sum to 2048; the longest is exactly 1024.
All inputs are finite; a program needn't handle non-finite values.
Results may differ from the reference program's by a relative error of at most 0.023.
Values may be sent and summed in bfloat16 or wider, within the bound.
No kernel may reach another device: no remote copies, remote signals or barrier semaphores. Data moves between devices by JAX's collectives and lax.ppermute only.
A program may use at most 64 MiB of HBM per device.

```python
import math
import jax
import jax.numpy as jnp
import numpy as np
from jax import lax

D = 8192
HD = 128
QH_DEV = 4
GROUP = 16
TOK_DEV = 256
SPAN = 4
HQ = 16
KVH = 1
TOKENS = 2048
NDOCS = 8
MAXDOC = 1024
N_CTX = 8
N_HEAD = 4


def shared_keys(key):
    return jnp.clip(jax.random.normal(key, (TOKENS, KVH * HD), jnp.float32), -4.0, 4.0)


def draw_key_rows(key, part):
    base = shared_keys(key)
    return base.astype(jnp.bfloat16)


def draw_queries(key, part):
    key = jax.random.fold_in(key, 7)
    own = jnp.clip(jax.random.normal(key, (TOKENS, HQ * HD), jnp.float32), -4.0, 4.0)
    return own.astype(jnp.bfloat16)


def level_of(rng, shape, cuts, smallest, largest):
    level, own = 1.0, jax.random.fold_in(rng, 6)
    for position, blocks in cuts:
        draws = jnp.exp(jax.random.uniform(jax.random.fold_in(own, position), (blocks,), jnp.float32, smallest / len(cuts), largest / len(cuts)))
        level = level * jnp.repeat(draws, shape[position] // blocks).reshape([-1 if axis == position else 1 for axis in range(len(shape))])
    return level


def split_up(amount, total, most, lean):
    loads = [(1 << 20) // math.isqrt(standing ** lean) + 1 for standing in range(2, amount + 1)]
    rest, counts = total - most - (amount - 1), [1] * (amount - 1)
    while rest > 0:
        free = [i for i in range(amount - 1) if counts[i] < most]
        whole, left = sum([loads[i] for i in free]), rest
        for i in free:
            extra = min(most - counts[i], max(1, left * loads[i] // whole), rest)
            counts[i] = counts[i] + extra
            rest = rest - extra
    return np.array([most] + counts)


def ragged(stream_key, number_of, total, bound, slope):
    if number_of == 2:
        one = jax.random.randint(stream_key, (), max(1, total - bound), min(bound, total - 1) + 1)
        return jnp.stack([one, total - one])
    sizes = jnp.asarray(split_up(number_of, total, bound, slope), jnp.int32)
    couples = (number_of - 1) // 2
    source_of, receiver = sizes[1:1 + 2 * couples:2], sizes[2:2 + 2 * couples:2]
    slack = jnp.minimum(source_of - 1, bound - receiver)
    moved = jax.random.randint(jax.random.fold_in(stream_key, 1), (couples,), 0, 1 << 20) % (slack + 1)
    sizes = sizes.at[1:1 + 2 * couples:2].set(source_of - moved).at[2:2 + 2 * couples:2].set(receiver + moved)
    return sizes[jax.random.permutation(jax.random.fold_in(stream_key, 2), number_of)]


def centred(stream_key, dims, spread, limit, shards=(), held_as=jnp.bfloat16):
    factor_of = level_of(stream_key, dims, shards, -0.22, 0.18) if shards else 1.0
    array = jax.random.normal(stream_key, dims, jnp.float32) * spread * factor_of
    return jnp.minimum(jnp.maximum(array, -limit), limit).astype(held_as)


def setup_inputs(seed: int = 0) -> dict:
    splits = jax.random.split(jax.random.key(seed), 6)
    return {
        "queries": draw_queries(jax.random.fold_in(splits[5], 71), 0),
        "key_rows": draw_key_rows(jax.random.fold_in(splits[5], 71), 0),
        "value_rows": centred(splits[2], (TOKENS, KVH * HD), 1.0, 6.0, ((0, 8),)),
        "lengths": ragged(splits[3], NDOCS, TOKENS, MAXDOC, 2).astype(jnp.int32),
        "out_weight": centred(splits[4], (HQ * HD, D), (HQ * HD) ** -0.5, 0.125, ((0, 4),)),
    }


def document_of(positions, doc_ends):
    return lax.optimization_barrier(jnp.sum((positions[:, None] >= doc_ends[None, :]).astype(jnp.int32), axis=1))

def reference(queries, key_rows, value_rows, lengths, out_weight):
    doc_ends = jnp.cumsum(lengths).astype(jnp.int32)
    reach = SPAN * TOK_DEV
    window = reach + TOK_DEV
    pad_keys = jnp.concatenate([jnp.zeros((reach, KVH * HD), key_rows.dtype), key_rows], axis=0)
    pad_values = jnp.concatenate([jnp.zeros((reach, KVH * HD), value_rows.dtype), value_rows], axis=0)
    inv_root = 1.0 / math.sqrt(HD)
    group_cols = QH_DEV * HD

    def one_block(block):
        first = (block * TOK_DEV).astype(jnp.int32)
        query_block = lax.dynamic_slice_in_dim(queries, first, TOK_DEV, 0).astype(jnp.float32).reshape(TOK_DEV, HQ, HD)
        key_block = lax.dynamic_slice_in_dim(pad_keys, first, window, 0).astype(jnp.float32).reshape(window, KVH, HD)
        value_block = lax.dynamic_slice_in_dim(pad_values, first, window, 0).astype(jnp.float32).reshape(window, KVH, HD)
        key_wide = jnp.repeat(key_block, GROUP, axis=1)
        value_wide = jnp.repeat(value_block, GROUP, axis=1)
        scores = jnp.einsum('qhd,khd->hqk', query_block, key_wide) * inv_root
        query_pos = first + jnp.arange(TOK_DEV, dtype=jnp.int32)
        key_pos = first - reach + jnp.arange(window, dtype=jnp.int32)
        same_doc = document_of(query_pos, doc_ends)[:, None] == document_of(key_pos, doc_ends)[None, :]
        allowed = same_doc & (key_pos[None, :] <= query_pos[:, None]) & (key_pos[None, :] >= 0)
        top_score = lax.optimization_barrier(jnp.max(jnp.where(allowed[None], scores, -1e+30), axis=2, keepdims=True))
        expo = jnp.where(allowed[None], jnp.exp(scores - top_score), 0.0)
        total = lax.optimization_barrier(jnp.sum(expo, axis=2))
        weights = lax.optimization_barrier(expo.astype(jnp.bfloat16)).astype(jnp.float32)
        summed = jnp.einsum('hqk,khd->qhd', weights, value_wide)
        attended = (summed / total.T[:, :, None]).astype(jnp.bfloat16).reshape(TOK_DEV, HQ * HD)

        def group_part(group):
            cols = lax.dynamic_slice_in_dim(attended, (group * group_cols).astype(jnp.int32), group_cols, 1)
            rows = lax.dynamic_slice_in_dim(out_weight, (group * group_cols).astype(jnp.int32), group_cols, 0)
            return jnp.dot(cols, rows, preferred_element_type=jnp.float32).astype(jnp.bfloat16)
        parts = lax.map(group_part, jnp.arange(N_HEAD, dtype=jnp.int32))
        return lax.optimization_barrier(jnp.sum(parts.astype(jnp.float32), axis=0)).astype(jnp.bfloat16)
    blocks = lax.map(one_block, jnp.arange(N_CTX, dtype=jnp.int32))
    return blocks.reshape(TOKENS, D)
```

```python
import functools
import math

import jax
import jax.numpy as jnp
from jax import lax
from jax.experimental import pallas as pl
from jax.experimental.pallas import tpu as pltpu
from jax.sharding import PartitionSpec as P

HD = 128
GROUP = 16
SPAN = 4
CORES = 2
MIB = 1024 * 1024

big_negative = -1e30
log2_scale = math.log2(math.e) / math.sqrt(HD)


def attention_kernel(place_ref, query_hbm, *refs):
    piece_refs, (out_ref, query_ref, sem) = refs[:-3], refs[-3:]
    query_copy = pltpu.make_async_copy(query_hbm, query_ref, sem)
    query_copy.start()
    rows = query_ref.shape[0]
    heads = query_ref.shape[1] // HD
    window = rows * len(piece_refs)
    first = place_ref[0]
    query_pos = first + lax.broadcasted_iota(jnp.int32, (rows, 1), 0)

    def step(d, carry):
        end, start = carry
        end = end + place_ref[1 + d]
        return end, jnp.where(query_pos >= end, end, start)

    _, doc_start = lax.fori_loop(
        0, place_ref.shape[0] - 1, step, (jnp.int32(0), jnp.zeros((rows, 1), jnp.int32))
    )
    key_pos = first - (window - rows) + lax.broadcasted_iota(jnp.int32, (rows, window), 1)
    allowed = (key_pos >= doc_start) & (key_pos <= query_pos)
    keys = jnp.concatenate([ref[:rows] for ref in piece_refs], axis=0)
    values = jnp.concatenate([ref[rows:] for ref in piece_refs], axis=0)
    query_copy.wait()
    for head in range(heads):
        query = query_ref[:, head * HD : (head + 1) * HD]
        scores = lax.dot_general(
            query, keys, (((1,), (1,)), ((), ())), preferred_element_type=jnp.float32
        )
        scores = jnp.where(allowed, scores * log2_scale, big_negative)
        top = jnp.max(scores, axis=1, keepdims=True)
        expo = jnp.where(allowed, jnp.exp2(scores - top), 0.0)
        total = jnp.sum(expo, axis=1, keepdims=True)
        summed = jnp.dot(expo.astype(jnp.bfloat16), values, preferred_element_type=jnp.float32)
        out_ref[:, head * HD : (head + 1) * HD] = (summed / total).astype(jnp.bfloat16)


def attention(queries, pieces, lengths, first_row):
    vmem = pl.BlockSpec(memory_space=pltpu.VMEM)
    return pl.pallas_call(
        attention_kernel,
        out_shape=jax.ShapeDtypeStruct(queries.shape, jnp.bfloat16),
        in_specs=[
            pl.BlockSpec(memory_space=pltpu.SMEM),
            pl.BlockSpec(memory_space=pltpu.HBM),
        ]
        + [vmem] * len(pieces),
        out_specs=vmem,
        scratch_shapes=[pltpu.VMEM(queries.shape, queries.dtype), pltpu.SemaphoreType.DMA],
        compiler_params=pltpu.CompilerParams(vmem_limit_bytes=24 * MIB),
        cost_estimate=pl.CostEstimate(flops=0, bytes_accessed=0, transcendentals=0),
        name="attention",
    )(jnp.concatenate([first_row[None], lengths]), queries, *pieces)


def tie(values, after):
    return lax.optimization_barrier((values, after))[0]


def chip_order(chips, core):
    bits = chips.bit_length() - 1
    return [
        sum(((k >> t) & 1) << (t if core == 0 else bits - 1 - t) for t in range(bits))
        for k in range(chips)
    ]


def plane_order(planes):
    order, mask = [0], planes - 1
    while mask:
        order += [x ^ mask for x in order]
        mask >>= 1
    return order


def project(attended, own_weight, weights, layout, half, place, chips):
    order = plane_order(sum(part.shape[0] for part in attended))
    planes = len(order)
    _, rows, depth = attended[0].shape
    cols = own_weight.shape[1] // CORES
    share = depth // chips
    rows_out = rows // planes
    block = min(cols, 256)
    size = (planes - 1) * depth
    aligned = share % HD == 0
    chip_orders = [chip_order(chips, core) for core in range(CORES)]
    operands = list(attended)
    if not aligned:
        others = jnp.concatenate(attended).reshape(planes, rows, chips, share)
        chip_index = place[1] ^ jnp.asarray(chip_orders)[(place[2] + half) % CORES]
        chip_index = chip_index[jnp.asarray([k for k, _ in layout])]
        plane_index = jnp.asarray([order.index(x) for _, x in layout])
        others = others.transpose(0, 2, 1, 3)[plane_index, chip_index]
        operands = [attended[0][0], others.transpose(1, 0, 2).reshape(rows, size)]

    def kernel(place_ref, *refs):
        attended_refs, refs = refs[: len(operands)], refs[len(operands) :]
        own_ref, refs = refs[0], refs[1:]
        weight_refs, refs = refs[: len(weights)], refs[len(weights) :]
        out_refs, (flat_ref, wide_ref) = refs[:planes], refs[planes:]
        head, chip = place_ref[0], place_ref[1]
        core = (place_ref[2] + half) % CORES

        blocks = [(ref, i) for ref in attended_refs for i in range(ref.shape[0])] * aligned
        for d, dest in enumerate(order):
            source = pl.ds(pl.multiple_of((head ^ dest) * rows_out, rows_out), rows_out)
            to = slice(d * rows_out, (d + 1) * rows_out)
            if not aligned:
                flat_ref[to, :] = attended_refs[0][source, :]
                wide_ref[to, :] = attended_refs[1][source, :]
                continue
            flat_ref[to, :] = attended_refs[0][0, source, :]
            for at, (k, x) in enumerate(layout):
                low, high = (chip_orders[c][k] for c in range(CORES))
                index = chip ^ (low + core * (high - low))
                column = pl.ds(pl.multiple_of(index * share, share), share)
                ref, i = blocks[order.index(x)]
                wide_ref[to, at * share : (at + 1) * share] = ref[i, source, column]

        for j in range(cols // block):
            columns = slice(j * block, (j + 1) * block)
            own = own_ref[:, pl.ds(pl.multiple_of(core * cols + j * block, HD), block)]
            acc = jnp.dot(flat_ref[...], own, preferred_element_type=jnp.float32)
            at = 0
            for ref in weight_refs:
                acc += jnp.dot(
                    wide_ref[:, at : at + ref.shape[0]],
                    ref[:, columns],
                    preferred_element_type=jnp.float32,
                )
                at += ref.shape[0]
            acc = acc.astype(jnp.bfloat16)
            for d, out_ref in enumerate(out_refs):
                out_ref[:, columns] = acc[d * rows_out : (d + 1) * rows_out]

    vmem = pl.BlockSpec(memory_space=pltpu.VMEM)
    return pl.pallas_call(
        kernel,
        out_shape=[jax.ShapeDtypeStruct((rows_out, cols), jnp.bfloat16)] * planes,
        in_specs=[pl.BlockSpec(memory_space=pltpu.SMEM)]
        + [vmem] * (len(operands) + 1 + len(weights)),
        out_specs=[vmem] * planes,
        scratch_shapes=[
            pltpu.VMEM((rows, depth), jnp.bfloat16),
            pltpu.VMEM((rows, size), jnp.bfloat16),
        ],
        compiler_params=pltpu.CompilerParams(vmem_limit_bytes=20 * MIB),
        cost_estimate=pl.CostEstimate(
            flops=2 * rows * planes * depth * cols,
            bytes_accessed=2 * (planes * depth * (rows + cols) + rows * cols),
            transcendentals=0,
        ),
        name="project",
    )(place, *operands, own_weight, *weights)


def assemble(pieces, half, width, place, out=None):
    order = plane_order(len(pieces))
    rows, cols = pieces[0].shape
    filled = [] if out is None else [out]

    def kernel(place_ref, *refs):
        out_ref, sem = refs[-2:]
        copies = []
        for k, x in enumerate(order):
            at = ((place_ref[0] ^ x) * CORES + (place_ref[2] + half) % CORES) * cols
            copies.append(
                pltpu.make_async_copy(
                    refs[k], out_ref.at[:, pl.ds(pl.multiple_of(at, HD), cols)], sem.at[k]
                )
            )
        for copy in copies:
            copy.start()
        for copy in copies:
            copy.wait()

    anywhere = pl.BlockSpec(memory_space=pl.ANY)
    return pl.pallas_call(
        kernel,
        out_shape=jax.ShapeDtypeStruct((rows, width), jnp.bfloat16),
        in_specs=[pl.BlockSpec(memory_space=pltpu.SMEM)]
        + [pl.BlockSpec(memory_space=pltpu.VMEM)] * len(pieces)
        + [anywhere] * len(filled),
        out_specs=anywhere,
        scratch_shapes=[pltpu.SemaphoreType.DMA((len(pieces),))],
        input_output_aliases={1 + len(pieces): 0} if filled else {},
        compiler_params=pltpu.CompilerParams(vmem_limit_bytes=4 * MIB),
        name="assemble",
    )(place, *pieces, *filled)


def paired(shard, x):
    length = lax.axis_size("head")
    return lax.ppermute(shard, "head", [(i, i ^ x) for i in range(length)])


def swapped(shard):
    length = lax.axis_size("ctx")
    return lax.ppermute(shard, "ctx", [(i, i ^ 1) for i in range(length)])


def crossed(shard, stage):
    length = lax.axis_size("ctx")
    bits = (length // CORES).bit_length() - 1
    bit = [stage, bits - 1 - stage]
    return lax.ppermute(
        shard, "ctx", [(i, i ^ (CORES << bit[i % CORES])) for i in range(length)]
    )


def later(shard, by):
    length = lax.axis_size("ctx")
    return lax.ppermute(shard, "ctx", [(i, i + by) for i in range(length - by)])


def body(queries, key_rows, value_rows, lengths, out_weight):
    rows = queries.shape[0]
    heads = queries.shape[1] // HD
    depth, width = out_weight.shape
    ctx, planes = lax.axis_size("ctx"), lax.axis_size("head")
    chips = ctx // CORES
    ctx_index, head_index = lax.axis_index("ctx"), lax.axis_index("head")
    chip, core = ctx_index // CORES, ctx_index % CORES
    share = depth // chips
    cols = width // (planes * CORES)
    place = jnp.stack([head_index, chip, core]).astype(jnp.int32)
    others = plane_order(planes)[1:]

    def share_of(x):
        column = ((head_index ^ x) * CORES + core) * cols
        return lax.dynamic_slice(out_weight, (chip * share, column), (share, cols))

    fetched = {x: paired(share_of(x), x) for x in others if x in (1, planes - 1)}
    for x in others:
        if x not in fetched:
            fetched[x] = paired(tie(share_of(x), fetched[planes - 1]), x)

    own = [key_rows, value_rows]
    if key_rows.shape[1] > HD:
        column = head_index * heads // GROUP * HD
        own = [lax.dynamic_slice_in_dim(part, column, HD, 1) for part in own]
    own = jnp.concatenate(own)
    late = tie(own, [fetched[1], fetched[planes - 1]])
    pieces = [later(own if d < 3 else late, d) for d in range(SPAN, 0, -1)] + [own]
    groups = [[1], [x for x in others if x > 1]]
    gathered = [fetched[1][None, None]]
    near = crossed(gathered[0], 0)
    attended = [attention(queries, pieces, lengths, ctx_index * rows)[None]]
    own_weight = lax.dynamic_slice_in_dim(
        tie(out_weight, attended), head_index * CORES * cols, CORES * cols, 1
    )

    shares, near, _ = lax.optimization_barrier(([fetched[x] for x in groups[1]], near, attended))
    gathered = [jnp.concatenate([gathered[0], near]), jnp.stack(shares)[None]]
    last = None
    plane_stages, chip_stages = planes.bit_length() - 1, chips.bit_length() - 1
    for stage in range(max(plane_stages, chip_stages)):
        new, near, far = [], [], []
        if stage < plane_stages:
            new = [paired(jnp.concatenate(attended), (planes - 1) >> stage)]
        if stage < chip_stages - 1:
            near = [crossed(gathered[0], stage + 1)]
        if stage < chip_stages:
            far = [crossed(gathered[1], stage)]
        new, near, far, own_weight = lax.optimization_barrier((new, near, far, own_weight))
        attended = attended + new
        gathered[0] = jnp.concatenate([gathered[0]] + near)
        if stage < chip_stages - 1:
            gathered[1] = jnp.concatenate([gathered[1]] + far)
        elif far:
            last = far[0]
    weights = [part.reshape(-1, cols) for part in gathered + [last]]
    layout = [(k, x) for k in range(chips) for x in groups[0]]
    layout += [(k, x) for k in range(chips) for x in groups[1]]

    result = project(attended, own_weight, weights, layout, 0, place, chips)
    moved = [result[0]] + [paired(part, x) for part, x in zip(result[1:], others)]
    weights = [swapped(part) for part in weights]
    out = assemble(moved, 0, width, place)
    result = project(attended, own_weight, weights, layout, 1, place, chips)
    moved = [result[0]] + [paired(part, x) for part, x in zip(result[1:], others)]
    return assemble(moved, 1, width, place, out)


def solution(mesh):
    placed = (P("ctx", "head"), P("ctx", None), P("ctx", None), P(), P("head", None))
    return jax.shard_map(
        body, mesh=mesh, in_specs=placed, out_specs=P(("ctx", "head"), None), check_vma=False
    )
```

```python
import functools
import math

import jax
import jax.numpy as jnp
from jax import lax
from jax.experimental import pallas as pl
from jax.experimental.pallas import tpu as pltpu
from jax.sharding import PartitionSpec as P

HD = 128
GROUP = 16
SPAN = 4
CORES = 2
MIB = 1024 * 1024

big_negative = -1e30
log2_scale = math.log2(math.e) / math.sqrt(HD)


def attention_kernel(place_ref, query_hbm, *refs):
    piece_refs, (out_ref, query_ref, sem) = refs[:-3], refs[-3:]
    query_copy = pltpu.make_async_copy(query_hbm, query_ref, sem)
    query_copy.start()
    rows = query_ref.shape[0]
    heads = query_ref.shape[1] // HD
    window = rows * len(piece_refs)
    first = place_ref[0]
    query_pos = first + lax.broadcasted_iota(jnp.int32, (rows, 1), 0)

    def step(d, carry):
        end, start = carry
        end = end + place_ref[1 + d]
        return end, jnp.where(query_pos >= end, end, start)

    _, doc_start = lax.fori_loop(
        0, place_ref.shape[0] - 1, step, (jnp.int32(0), jnp.zeros((rows, 1), jnp.int32))
    )
    key_pos = first - (window - rows) + lax.broadcasted_iota(jnp.int32, (rows, window), 1)
    allowed = (key_pos >= doc_start) & (key_pos <= query_pos)
    keys = jnp.concatenate([ref[:rows] for ref in piece_refs], axis=0)
    values = jnp.concatenate([ref[rows:] for ref in piece_refs], axis=0)
    query_copy.wait()
    for head in range(heads):
        query = query_ref[:, head * HD : (head + 1) * HD]
        scores = lax.dot_general(
            query, keys, (((1,), (1,)), ((), ())), preferred_element_type=jnp.float32
        )
        scores = jnp.where(allowed, scores * log2_scale, big_negative)
        top = jnp.max(scores, axis=1, keepdims=True)
        expo = jnp.where(allowed, jnp.exp2(scores - top), 0.0)
        total = jnp.sum(expo, axis=1, keepdims=True)
        summed = jnp.dot(expo.astype(jnp.bfloat16), values, preferred_element_type=jnp.float32)
        out_ref[:, head * HD : (head + 1) * HD] = (summed / total).astype(jnp.bfloat16)


def attention(queries, pieces, lengths, first_row):
    vmem = pl.BlockSpec(memory_space=pltpu.VMEM)
    return pl.pallas_call(
        attention_kernel,
        out_shape=jax.ShapeDtypeStruct(queries.shape, jnp.bfloat16),
        in_specs=[
            pl.BlockSpec(memory_space=pltpu.SMEM),
            pl.BlockSpec(memory_space=pltpu.HBM),
        ]
        + [vmem] * len(pieces),
        out_specs=vmem,
        scratch_shapes=[pltpu.VMEM(queries.shape, queries.dtype), pltpu.SemaphoreType.DMA],
        compiler_params=pltpu.CompilerParams(vmem_limit_bytes=24 * MIB),
        cost_estimate=pl.CostEstimate(flops=0, bytes_accessed=0, transcendentals=0),
        name="attention",
    )(jnp.concatenate([first_row[None], lengths]), queries, *pieces)


def tie(values, after):
    return lax.optimization_barrier((values, after))[0]


def chip_order(chips, core):
    bits = chips.bit_length() - 1
    return [
        sum(((k >> t) & 1) << (t if core == 0 else bits - 1 - t) for t in range(bits))
        for k in range(chips)
    ]


def plane_order(planes):
    order, mask = [0], planes - 1
    while mask:
        order += [x ^ mask for x in order]
        mask >>= 1
    return order


def project(attended, own_weight, weights, layout, half, place, chips):
    order = plane_order(sum(part.shape[0] for part in attended))
    planes = len(order)
    _, rows, depth = attended[0].shape
    cols = own_weight.shape[1] // CORES
    share = depth // chips
    rows_out = rows // planes
    block = min(cols, 256)
    size = (planes - 1) * depth
    aligned = share % HD == 0
    chip_orders = [chip_order(chips, core) for core in range(CORES)]
    operands = list(attended)
    if not aligned:
        others = jnp.concatenate(attended).reshape(planes, rows, chips, share)
        chip_index = place[1] ^ jnp.asarray(chip_orders)[(place[2] + half) % CORES]
        chip_index = chip_index[jnp.asarray([k for k, _ in layout])]
        plane_index = jnp.asarray([order.index(x) for _, x in layout])
        others = others.transpose(0, 2, 1, 3)[plane_index, chip_index]
        operands = [attended[0][0], others.transpose(1, 0, 2).reshape(rows, size)]

    def kernel(place_ref, *refs):
        attended_refs, refs = refs[: len(operands)], refs[len(operands) :]
        own_ref, refs = refs[0], refs[1:]
        weight_refs, refs = refs[: len(weights)], refs[len(weights) :]
        out_refs, (flat_ref, wide_ref) = refs[:planes], refs[planes:]
        head, chip = place_ref[0], place_ref[1]
        core = (place_ref[2] + half) % CORES

        blocks = [(ref, i) for ref in attended_refs for i in range(ref.shape[0])] * aligned
        for d, dest in enumerate(order):
            source = pl.ds(pl.multiple_of((head ^ dest) * rows_out, rows_out), rows_out)
            to = slice(d * rows_out, (d + 1) * rows_out)
            if not aligned:
                flat_ref[to, :] = attended_refs[0][source, :]
                wide_ref[to, :] = attended_refs[1][source, :]
                continue
            flat_ref[to, :] = attended_refs[0][0, source, :]
            for at, (k, x) in enumerate(layout):
                low, high = (chip_orders[c][k] for c in range(CORES))
                index = chip ^ (low + core * (high - low))
                column = pl.ds(pl.multiple_of(index * share, share), share)
                ref, i = blocks[order.index(x)]
                wide_ref[to, at * share : (at + 1) * share] = ref[i, source, column]

        for j in range(cols // block):
            columns = slice(j * block, (j + 1) * block)
            own = own_ref[:, pl.ds(pl.multiple_of(core * cols + j * block, HD), block)]
            acc = jnp.dot(flat_ref[...], own, preferred_element_type=jnp.float32)
            at = 0
            for ref in weight_refs:
                acc += jnp.dot(
                    wide_ref[:, at : at + ref.shape[0]],
                    ref[:, columns],
                    preferred_element_type=jnp.float32,
                )
                at += ref.shape[0]
            acc = acc.astype(jnp.bfloat16)
            for d, out_ref in enumerate(out_refs):
                out_ref[:, columns] = acc[d * rows_out : (d + 1) * rows_out]

    vmem = pl.BlockSpec(memory_space=pltpu.VMEM)
    return pl.pallas_call(
        kernel,
        out_shape=[jax.ShapeDtypeStruct((rows_out, cols), jnp.bfloat16)] * planes,
        in_specs=[pl.BlockSpec(memory_space=pltpu.SMEM)]
        + [vmem] * (len(operands) + 1 + len(weights)),
        out_specs=[vmem] * planes,
        scratch_shapes=[
            pltpu.VMEM((rows, depth), jnp.bfloat16),
            pltpu.VMEM((rows, size), jnp.bfloat16),
        ],
        compiler_params=pltpu.CompilerParams(vmem_limit_bytes=20 * MIB),
        cost_estimate=pl.CostEstimate(
            flops=2 * rows * planes * depth * cols,
            bytes_accessed=2 * (planes * depth * (rows + cols) + rows * cols),
            transcendentals=0,
        ),
        name="project",
    )(place, *operands, own_weight, *weights)


def assemble(pieces, half, width, place, out=None):
    order = plane_order(len(pieces))
    rows, cols = pieces[0].shape
    filled = [] if out is None else [out]

    def kernel(place_ref, *refs):
        out_ref, sem = refs[-2:]
        copies = []
        for k, x in enumerate(order):
            at = ((place_ref[0] ^ x) * CORES + (place_ref[2] + half) % CORES) * cols
            copies.append(
                pltpu.make_async_copy(
                    refs[k], out_ref.at[:, pl.ds(pl.multiple_of(at, HD), cols)], sem.at[k]
                )
            )
        for copy in copies:
            copy.start()
        for copy in copies:
            copy.wait()

    anywhere = pl.BlockSpec(memory_space=pl.ANY)
    return pl.pallas_call(
        kernel,
        out_shape=jax.ShapeDtypeStruct((rows, width), jnp.bfloat16),
        in_specs=[pl.BlockSpec(memory_space=pltpu.SMEM)]
        + [pl.BlockSpec(memory_space=pltpu.VMEM)] * len(pieces)
        + [anywhere] * len(filled),
        out_specs=anywhere,
        scratch_shapes=[pltpu.SemaphoreType.DMA((len(pieces),))],
        input_output_aliases={1 + len(pieces): 0} if filled else {},
        compiler_params=pltpu.CompilerParams(vmem_limit_bytes=4 * MIB),
        name="assemble",
    )(place, *pieces, *filled)


def paired(shard, x):
    length = lax.axis_size("head")
    return lax.ppermute(shard, "head", [(i, i ^ x) for i in range(length)])


def swapped(shard):
    length = lax.axis_size("ctx")
    return lax.ppermute(shard, "ctx", [(i, i ^ 1) for i in range(length)])


def crossed(shard, stage):
    length = lax.axis_size("ctx")
    bits = (length // CORES).bit_length() - 1
    bit = [stage, bits - 1 - stage]
    return lax.ppermute(
        shard, "ctx", [(i, i ^ (CORES << bit[i % CORES])) for i in range(length)]
    )


def later(shard, by):
    length = lax.axis_size("ctx")
    return lax.ppermute(shard, "ctx", [(i, i + by) for i in range(length - by)])


def body(queries, key_rows, value_rows, lengths, out_weight):
    rows = queries.shape[0]
    heads = queries.shape[1] // HD
    depth, width = out_weight.shape
    ctx, planes = lax.axis_size("ctx"), lax.axis_size("head")
    chips = ctx // CORES
    ctx_index, head_index = lax.axis_index("ctx"), lax.axis_index("head")
    chip, core = ctx_index // CORES, ctx_index % CORES
    share = depth // chips
    cols = width // (planes * CORES)
    place = jnp.stack([head_index, chip, core]).astype(jnp.int32)
    others = plane_order(planes)[1:]

    def share_of(x):
        column = ((head_index ^ x) * CORES + core) * cols
        return lax.dynamic_slice(out_weight, (chip * share, column), (share, cols))

    fetched = {x: paired(share_of(x), x) for x in others if x in (1, planes - 1)}
    own = [key_rows, value_rows]
    if key_rows.shape[1] > HD:
        column = head_index * heads // GROUP * HD
        own = [lax.dynamic_slice_in_dim(part, column, HD, 1) for part in own]
    own = jnp.concatenate(own)
    pieces = [later(own, d) for d in range(SPAN, 0, -1)] + [own]
    for x in others:
        if x not in fetched:
            fetched[x] = paired(tie(share_of(x), (fetched[planes - 1], pieces[1:-1])), x)
    groups = [[x for x in others if x in (1, planes - 1)]]
    groups.append([x for x in others if x not in groups[0]])
    plane_stages, chip_stages = planes.bit_length() - 1, chips.bit_length() - 1
    first = jnp.stack(tie([fetched[x] for x in groups[0]], pieces[1:-1]))[None]
    first = jnp.concatenate([first, crossed(first, 0)])
    pieces, first = lax.optimization_barrier((pieces, first))
    rest = crossed(first, 1)
    attended = [attention(queries, pieces, lengths, ctx_index * rows)[None]]
    own_weight = lax.dynamic_slice_in_dim(
        tie(out_weight, attended), head_index * CORES * cols, CORES * cols, 1
    )

    second = jnp.stack(tie([fetched[x] for x in groups[1]], (attended, first)))[None]
    early, latest = [], attended
    for stage in range(max(plane_stages, chip_stages)):
        ahead, new, more = [], [], []
        if stage < plane_stages:
            new = [paired(jnp.concatenate(latest), (planes - 1) >> stage)]
        if stage + 1 < plane_stages:
            ahead = [paired(jnp.concatenate(attended), (planes - 1) >> (stage + 1))]
        if stage < chip_stages:
            more = [crossed(second, stage)]
        ahead, new, more, own_weight = lax.optimization_barrier((ahead, new, more, own_weight))
        latest = early + new
        attended, early = attended + latest, ahead
        second = jnp.concatenate([second] + more)
        if stage > 0 and stage + 1 < chip_stages:
            first, rest = jnp.concatenate([first, rest]), None
            rest = crossed(first, stage + 1)
    weights = [part.reshape(-1, cols) for part in (first, rest, second)]
    layout = [(k, x) for k in range(chips) for x in groups[0]]
    layout += [(k, x) for k in range(chips) for x in groups[1]]

    result = project(attended, own_weight, weights, layout, 0, place, chips)
    moved = [result[0]] + [paired(part, x) for part, x in zip(result[1:], others)]
    weights = [swapped(part) for part in weights]
    out = assemble(moved, 0, width, place)
    result = project(attended, own_weight, weights, layout, 1, place, chips)
    moved = [result[0]] + [paired(part, x) for part, x in zip(result[1:], others)]
    return assemble(moved, 1, width, place, out)


def solution(mesh):
    placed = (P("ctx", "head"), P("ctx", None), P("ctx", None), P(), P("head", None))
    return jax.shard_map(
        body, mesh=mesh, in_specs=placed, out_specs=P(("ctx", "head"), None), check_vma=False
    )
```

```python
import functools
import math

import jax
import jax.numpy as jnp
from jax import lax
from jax.experimental import pallas as pl
from jax.experimental.pallas import tpu as pltpu
from jax.sharding import PartitionSpec as P

HD = 128
GROUP = 16
SPAN = 4
CORES = 2
MIB = 1024 * 1024

big_negative = -1e30
log2_scale = math.log2(math.e) / math.sqrt(HD)


def attention_kernel(place_ref, query_hbm, *refs):
    piece_refs, (out_ref, query_ref, sem) = refs[:-3], refs[-3:]
    query_copy = pltpu.make_async_copy(query_hbm, query_ref, sem)
    query_copy.start()
    rows = query_ref.shape[0]
    heads = query_ref.shape[1] // HD
    window = rows * len(piece_refs)
    first = place_ref[0]
    query_pos = first + lax.broadcasted_iota(jnp.int32, (rows, 1), 0)

    def step(d, carry):
        end, start = carry
        end = end + place_ref[1 + d]
        return end, jnp.where(query_pos >= end, end, start)

    _, doc_start = lax.fori_loop(
        0, place_ref.shape[0] - 1, step, (jnp.int32(0), jnp.zeros((rows, 1), jnp.int32))
    )
    key_pos = first - (window - rows) + lax.broadcasted_iota(jnp.int32, (rows, window), 1)
    allowed = (key_pos >= doc_start) & (key_pos <= query_pos)
    keys = jnp.concatenate([ref[:rows] for ref in piece_refs], axis=0)
    values = jnp.concatenate([ref[rows:] for ref in piece_refs], axis=0)
    query_copy.wait()
    for head in range(heads):
        query = query_ref[:, head * HD : (head + 1) * HD]
        scores = lax.dot_general(
            query, keys, (((1,), (1,)), ((), ())), preferred_element_type=jnp.float32
        )
        scores = jnp.where(allowed, scores * log2_scale, big_negative)
        top = jnp.max(scores, axis=1, keepdims=True)
        expo = jnp.where(allowed, jnp.exp2(scores - top), 0.0)
        total = jnp.sum(expo, axis=1, keepdims=True)
        summed = jnp.dot(expo.astype(jnp.bfloat16), values, preferred_element_type=jnp.float32)
        out_ref[:, head * HD : (head + 1) * HD] = (summed / total).astype(jnp.bfloat16)


def attention(queries, pieces, lengths, first_row):
    vmem = pl.BlockSpec(memory_space=pltpu.VMEM)
    return pl.pallas_call(
        attention_kernel,
        out_shape=jax.ShapeDtypeStruct(queries.shape, jnp.bfloat16),
        in_specs=[
            pl.BlockSpec(memory_space=pltpu.SMEM),
            pl.BlockSpec(memory_space=pltpu.HBM),
        ]
        + [vmem] * len(pieces),
        out_specs=vmem,
        scratch_shapes=[pltpu.VMEM(queries.shape, queries.dtype), pltpu.SemaphoreType.DMA],
        compiler_params=pltpu.CompilerParams(vmem_limit_bytes=24 * MIB),
        cost_estimate=pl.CostEstimate(flops=0, bytes_accessed=0, transcendentals=0),
        name="attention",
    )(jnp.concatenate([first_row[None], lengths]), queries, *pieces)


def tie(values, after):
    return lax.optimization_barrier((values, after))[0]


def chip_order(chips, core):
    bits = chips.bit_length() - 1
    return [
        sum(((k >> t) & 1) << (t if core == 0 else bits - 1 - t) for t in range(bits))
        for k in range(chips)
    ]


def plane_order(planes):
    order, mask = [0], planes - 1
    while mask:
        order += [x ^ mask for x in order]
        mask >>= 1
    return order


def project(attended, own_weight, weights, layout, half, place, chips):
    order = plane_order(sum(part.shape[0] for part in attended))
    planes = len(order)
    _, rows, depth = attended[0].shape
    cols = own_weight.shape[1] // CORES
    share = depth // chips
    rows_out = rows // planes
    block = min(cols, 256)
    size = (planes - 1) * depth
    aligned = share % HD == 0
    chip_orders = [chip_order(chips, core) for core in range(CORES)]
    operands = list(attended)
    if not aligned:
        others = jnp.concatenate(attended).reshape(planes, rows, chips, share)
        chip_index = place[1] ^ jnp.asarray(chip_orders)[(place[2] + half) % CORES]
        chip_index = chip_index[jnp.asarray([k for k, _ in layout])]
        plane_index = jnp.asarray([order.index(x) for _, x in layout])
        others = others.transpose(0, 2, 1, 3)[plane_index, chip_index]
        operands = [attended[0][0], others.transpose(1, 0, 2).reshape(rows, size)]

    def kernel(place_ref, *refs):
        attended_refs, refs = refs[: len(operands)], refs[len(operands) :]
        own_ref, refs = refs[0], refs[1:]
        weight_refs, refs = refs[: len(weights)], refs[len(weights) :]
        out_refs, (flat_ref, wide_ref) = refs[:planes], refs[planes:]
        head, chip = place_ref[0], place_ref[1]
        core = (place_ref[2] + half) % CORES

        blocks = [(ref, i) for ref in attended_refs for i in range(ref.shape[0])] * aligned
        for d, dest in enumerate(order):
            source = pl.ds(pl.multiple_of((head ^ dest) * rows_out, rows_out), rows_out)
            to = slice(d * rows_out, (d + 1) * rows_out)
            if not aligned:
                flat_ref[to, :] = attended_refs[0][source, :]
                wide_ref[to, :] = attended_refs[1][source, :]
                continue
            flat_ref[to, :] = attended_refs[0][0, source, :]
            for at, (k, x) in enumerate(layout):
                low, high = (chip_orders[c][k] for c in range(CORES))
                index = chip ^ (low + core * (high - low))
                column = pl.ds(pl.multiple_of(index * share, share), share)
                ref, i = blocks[order.index(x)]
                wide_ref[to, at * share : (at + 1) * share] = ref[i, source, column]

        for j in range(cols // block):
            columns = slice(j * block, (j + 1) * block)
            own = own_ref[:, pl.ds(pl.multiple_of(core * cols + j * block, HD), block)]
            acc = jnp.dot(flat_ref[...], own, preferred_element_type=jnp.float32)
            at = 0
            for ref in weight_refs:
                acc += jnp.dot(
                    wide_ref[:, at : at + ref.shape[0]],
                    ref[:, columns],
                    preferred_element_type=jnp.float32,
                )
                at += ref.shape[0]
            acc = acc.astype(jnp.bfloat16)
            for d, out_ref in enumerate(out_refs):
                out_ref[:, columns] = acc[d * rows_out : (d + 1) * rows_out]

    vmem = pl.BlockSpec(memory_space=pltpu.VMEM)
    return pl.pallas_call(
        kernel,
        out_shape=[jax.ShapeDtypeStruct((rows_out, cols), jnp.bfloat16)] * planes,
        in_specs=[pl.BlockSpec(memory_space=pltpu.SMEM)]
        + [vmem] * (len(operands) + 1 + len(weights)),
        out_specs=[vmem] * planes,
        scratch_shapes=[
            pltpu.VMEM((rows, depth), jnp.bfloat16),
            pltpu.VMEM((rows, size), jnp.bfloat16),
        ],
        compiler_params=pltpu.CompilerParams(vmem_limit_bytes=20 * MIB),
        cost_estimate=pl.CostEstimate(
            flops=2 * rows * planes * depth * cols,
            bytes_accessed=2 * (planes * depth * (rows + cols) + rows * cols),
            transcendentals=0,
        ),
        name="project",
    )(place, *operands, own_weight, *weights)


def assemble(pieces, half, width, place, out=None):
    order = plane_order(len(pieces))
    rows, cols = pieces[0].shape
    filled = [] if out is None else [out]

    def kernel(place_ref, *refs):
        out_ref, sem = refs[-2:]
        copies = []
        for k, x in enumerate(order):
            at = ((place_ref[0] ^ x) * CORES + (place_ref[2] + half) % CORES) * cols
            copies.append(
                pltpu.make_async_copy(
                    refs[k], out_ref.at[:, pl.ds(pl.multiple_of(at, HD), cols)], sem.at[k]
                )
            )
        for copy in copies:
            copy.start()
        for copy in copies:
            copy.wait()

    anywhere = pl.BlockSpec(memory_space=pl.ANY)
    return pl.pallas_call(
        kernel,
        out_shape=jax.ShapeDtypeStruct((rows, width), jnp.bfloat16),
        in_specs=[pl.BlockSpec(memory_space=pltpu.SMEM)]
        + [pl.BlockSpec(memory_space=pltpu.VMEM)] * len(pieces)
        + [anywhere] * len(filled),
        out_specs=anywhere,
        scratch_shapes=[pltpu.SemaphoreType.DMA((len(pieces),))],
        input_output_aliases={1 + len(pieces): 0} if filled else {},
        compiler_params=pltpu.CompilerParams(vmem_limit_bytes=4 * MIB),
        name="assemble",
    )(place, *pieces, *filled)


def paired(shard, x):
    length = lax.axis_size("head")
    return lax.ppermute(shard, "head", [(i, i ^ x) for i in range(length)])


def swapped(shard):
    length = lax.axis_size("ctx")
    return lax.ppermute(shard, "ctx", [(i, i ^ 1) for i in range(length)])


def crossed(shard, stage):
    length = lax.axis_size("ctx")
    bits = (length // CORES).bit_length() - 1
    bit = [stage, bits - 1 - stage]
    return lax.ppermute(
        shard, "ctx", [(i, i ^ (CORES << bit[i % CORES])) for i in range(length)]
    )


def later(shard, by):
    length = lax.axis_size("ctx")
    return lax.ppermute(shard, "ctx", [(i, i + by) for i in range(length - by)])


def body(queries, key_rows, value_rows, lengths, out_weight):
    rows = queries.shape[0]
    heads = queries.shape[1] // HD
    depth, width = out_weight.shape
    ctx, planes = lax.axis_size("ctx"), lax.axis_size("head")
    chips = ctx // CORES
    ctx_index, head_index = lax.axis_index("ctx"), lax.axis_index("head")
    chip, core = ctx_index // CORES, ctx_index % CORES
    share = depth // chips
    cols = width // (planes * CORES)
    place = jnp.stack([head_index, chip, core]).astype(jnp.int32)
    others = plane_order(planes)[1:]

    def share_of(x):
        column = ((head_index ^ x) * CORES + core) * cols
        return lax.dynamic_slice(out_weight, (chip * share, column), (share, cols))

    fetched = {x: paired(share_of(x), x) for x in others if x in (1, planes - 1)}
    own = [key_rows, value_rows]
    if key_rows.shape[1] > HD:
        column = head_index * heads // GROUP * HD
        own = [lax.dynamic_slice_in_dim(part, column, HD, 1) for part in own]
    own = jnp.concatenate(own)
    late = tie(own, fetched[1])
    pieces = [later(own if d < SPAN else late, d) for d in range(SPAN, 0, -1)] + [own]
    for x in others:
        if x not in fetched:
            fetched[x] = paired(tie(share_of(x), (fetched[planes - 1], pieces[2:-1])), x)
    groups = [[x for x in others if x in (1, planes - 1)]]
    groups.append([x for x in others if x not in groups[0]])
    plane_stages, chip_stages = planes.bit_length() - 1, chips.bit_length() - 1
    first = jnp.stack(tie([fetched[x] for x in groups[0]], pieces[2:-1]))[None]
    first = jnp.concatenate([first, crossed(first, 0)])
    rest = crossed(first, 1)
    attended = [attention(queries, pieces, lengths, ctx_index * rows)[None]]
    middle = [fetched[x] for x in groups[1]]
    attended, middle = lax.optimization_barrier((attended, middle))
    own_weight = lax.dynamic_slice_in_dim(
        tie(out_weight, attended), head_index * CORES * cols, CORES * cols, 1
    )

    second = jnp.stack(tie(middle, first))[None]
    early, latest = [], attended
    for stage in range(max(plane_stages, chip_stages)):
        ahead, new, more = [], [], []
        if stage < plane_stages:
            new = [paired(jnp.concatenate(latest), (planes - 1) >> stage)]
        if stage + 1 < plane_stages:
            ahead = [paired(jnp.concatenate(attended), (planes - 1) >> (stage + 1))]
        if stage < chip_stages:
            more = [crossed(second, stage)]
        ahead, new, more, own_weight = lax.optimization_barrier((ahead, new, more, own_weight))
        latest = early + new
        attended, early = attended + latest, ahead
        second = jnp.concatenate([second] + more)
        if stage > 0 and stage + 1 < chip_stages:
            first, rest = jnp.concatenate([first, rest]), None
            rest = crossed(first, stage + 1)
    weights = [part.reshape(-1, cols) for part in (first, rest, second)]
    layout = [(k, x) for k in range(chips) for x in groups[0]]
    layout += [(k, x) for k in range(chips) for x in groups[1]]

    result = project(attended, own_weight, weights, layout, 0, place, chips)
    moved = [result[0]] + [paired(part, x) for part, x in zip(result[1:], others)]
    weights = [swapped(part) for part in weights]
    out = assemble(moved, 0, width, place)
    result = project(attended, own_weight, weights, layout, 1, place, chips)
    moved = [result[0]] + [paired(part, x) for part, x in zip(result[1:], others)]
    return assemble(moved, 1, width, place, out)


def solution(mesh):
    placed = (P("ctx", "head"), P("ctx", None), P("ctx", None), P(), P("head", None))
    return jax.shard_map(
        body, mesh=mesh, in_specs=placed, out_specs=P(("ctx", "head"), None), check_vma=False
    )
```

```python
import functools
import math

import jax
import jax.numpy as jnp
from jax import lax
from jax.experimental import pallas as pl
from jax.experimental.pallas import tpu as pltpu
from jax.sharding import PartitionSpec as P

HD = 128
GROUP = 16
SPAN = 4
CORES = 2
MIB = 1024 * 1024

big_negative = -1e30
log2_scale = math.log2(math.e) / math.sqrt(HD)


def attention_kernel(place_ref, query_hbm, *refs):
    piece_refs, (out_ref, query_ref, sem) = refs[:-3], refs[-3:]
    query_copy = pltpu.make_async_copy(query_hbm, query_ref, sem)
    query_copy.start()
    rows = query_ref.shape[0]
    heads = query_ref.shape[1] // HD
    window = rows * len(piece_refs)
    first = place_ref[0]
    query_pos = first + lax.broadcasted_iota(jnp.int32, (rows, 1), 0)

    def step(d, carry):
        end, start = carry
        end = end + place_ref[1 + d]
        return end, jnp.where(query_pos >= end, end, start)

    _, doc_start = lax.fori_loop(
        0, place_ref.shape[0] - 1, step, (jnp.int32(0), jnp.zeros((rows, 1), jnp.int32))
    )
    key_pos = first - (window - rows) + lax.broadcasted_iota(jnp.int32, (rows, window), 1)
    allowed = (key_pos >= doc_start) & (key_pos <= query_pos)
    keys = jnp.concatenate([ref[:rows] for ref in piece_refs], axis=0)
    values = jnp.concatenate([ref[rows:] for ref in piece_refs], axis=0)
    query_copy.wait()
    for head in range(heads):
        query = query_ref[:, head * HD : (head + 1) * HD]
        scores = lax.dot_general(
            query, keys, (((1,), (1,)), ((), ())), preferred_element_type=jnp.float32
        )
        scores = jnp.where(allowed, scores * log2_scale, big_negative)
        top = jnp.max(scores, axis=1, keepdims=True)
        expo = jnp.exp2(scores - top)
        total = jnp.sum(expo, axis=1, keepdims=True)
        summed = jnp.dot(expo.astype(jnp.bfloat16), values, preferred_element_type=jnp.float32)
        out_ref[:, head * HD : (head + 1) * HD] = (summed / total).astype(jnp.bfloat16)


def attention(queries, pieces, lengths, first_row):
    vmem = pl.BlockSpec(memory_space=pltpu.VMEM)
    return pl.pallas_call(
        attention_kernel,
        out_shape=jax.ShapeDtypeStruct(queries.shape, jnp.bfloat16),
        in_specs=[
            pl.BlockSpec(memory_space=pltpu.SMEM),
            pl.BlockSpec(memory_space=pltpu.HBM),
        ]
        + [vmem] * len(pieces),
        out_specs=vmem,
        scratch_shapes=[pltpu.VMEM(queries.shape, queries.dtype), pltpu.SemaphoreType.DMA],
        compiler_params=pltpu.CompilerParams(vmem_limit_bytes=24 * MIB),
        cost_estimate=pl.CostEstimate(flops=0, bytes_accessed=0, transcendentals=0),
        name="attention",
    )(jnp.concatenate([first_row[None], lengths]), queries, *pieces)


def tie(values, after):
    return lax.optimization_barrier((values, after))[0]


def chip_order(chips, core):
    bits = chips.bit_length() - 1
    return [
        sum(((k >> t) & 1) << (t if core == 0 else bits - 1 - t) for t in range(bits))
        for k in range(chips)
    ]


def plane_order(planes):
    order, mask = [0], planes - 1
    while mask:
        order += [x ^ mask for x in order]
        mask >>= 1
    return order


def project(attended, own_weight, weights, layout, half, place, chips):
    order = plane_order(sum(part.shape[0] for part in attended))
    planes = len(order)
    _, rows, depth = attended[0].shape
    cols = own_weight.shape[1] // CORES
    share = depth // chips
    rows_out = rows // planes
    block = min(cols, 512)
    size = (planes - 1) * depth
    aligned = share % HD == 0
    chip_orders = [chip_order(chips, core) for core in range(CORES)]
    operands = list(attended)
    if not aligned:
        others = jnp.concatenate(attended).reshape(planes, rows, chips, share)
        chip_index = place[1] ^ jnp.asarray(chip_orders)[(place[2] + half) % CORES]
        chip_index = chip_index[jnp.asarray([k for k, _ in layout])]
        plane_index = jnp.asarray([order.index(x) for _, x in layout])
        others = others.transpose(0, 2, 1, 3)[plane_index, chip_index]
        operands = [attended[0][0], others.transpose(1, 0, 2).reshape(rows, size)]

    def kernel(place_ref, *refs):
        attended_refs, refs = refs[: len(operands)], refs[len(operands) :]
        own_ref, refs = refs[0], refs[1:]
        weight_refs, refs = refs[: len(weights)], refs[len(weights) :]
        out_refs, (flat_ref, wide_ref) = refs[:planes], refs[planes:]
        head, chip = place_ref[0], place_ref[1]
        core = (place_ref[2] + half) % CORES

        blocks = [(ref, i) for ref in attended_refs for i in range(ref.shape[0])] * aligned
        for d, dest in enumerate(order):
            source = pl.ds(pl.multiple_of((head ^ dest) * rows_out, rows_out), rows_out)
            to = slice(d * rows_out, (d + 1) * rows_out)
            if not aligned:
                flat_ref[to, :] = attended_refs[0][source, :]
                wide_ref[to, :] = attended_refs[1][source, :]
                continue
            flat_ref[to, :] = attended_refs[0][0, source, :]
            for at, (k, x) in enumerate(layout):
                low, high = (chip_orders[c][k] for c in range(CORES))
                index = chip ^ (low + core * (high - low))
                column = pl.ds(pl.multiple_of(index * share, share), share)
                ref, i = blocks[order.index(x)]
                wide_ref[to, at * share : (at + 1) * share] = ref[i, source, column]

        for j in range(cols // block):
            columns = slice(j * block, (j + 1) * block)
            own = own_ref[:, pl.ds(pl.multiple_of(core * cols + j * block, HD), block)]
            acc = jnp.dot(flat_ref[...], own, preferred_element_type=jnp.float32)
            at = 0
            for ref in weight_refs:
                acc += jnp.dot(
                    wide_ref[:, at : at + ref.shape[0]],
                    ref[:, columns],
                    preferred_element_type=jnp.float32,
                )
                at += ref.shape[0]
            acc = acc.astype(jnp.bfloat16)
            for d, out_ref in enumerate(out_refs):
                out_ref[:, columns] = acc[d * rows_out : (d + 1) * rows_out]

    vmem = pl.BlockSpec(memory_space=pltpu.VMEM)
    return pl.pallas_call(
        kernel,
        out_shape=[jax.ShapeDtypeStruct((rows_out, cols), jnp.bfloat16)] * planes,
        in_specs=[pl.BlockSpec(memory_space=pltpu.SMEM)]
        + [vmem] * (len(operands) + 1 + len(weights)),
        out_specs=[vmem] * planes,
        scratch_shapes=[
            pltpu.VMEM((rows, depth), jnp.bfloat16),
            pltpu.VMEM((rows, size), jnp.bfloat16),
        ],
        compiler_params=pltpu.CompilerParams(vmem_limit_bytes=20 * MIB),
        cost_estimate=pl.CostEstimate(
            flops=2 * rows * planes * depth * cols,
            bytes_accessed=2 * (planes * depth * (rows + cols) + rows * cols),
            transcendentals=0,
        ),
        name="project",
    )(place, *operands, own_weight, *weights)


def assemble(pieces, half, width, place, out=None):
    order = plane_order(len(pieces))
    rows, cols = pieces[0].shape
    filled = [] if out is None else [out]

    def kernel(place_ref, *refs):
        out_ref, sem = refs[-2:]
        copies = []
        for k, x in enumerate(order):
            at = ((place_ref[0] ^ x) * CORES + (place_ref[2] + half) % CORES) * cols
            copies.append(
                pltpu.make_async_copy(
                    refs[k], out_ref.at[:, pl.ds(pl.multiple_of(at, HD), cols)], sem.at[k]
                )
            )
        for copy in copies:
            copy.start()
        for copy in copies:
            copy.wait()

    anywhere = pl.BlockSpec(memory_space=pl.ANY)
    return pl.pallas_call(
        kernel,
        out_shape=jax.ShapeDtypeStruct((rows, width), jnp.bfloat16),
        in_specs=[pl.BlockSpec(memory_space=pltpu.SMEM)]
        + [pl.BlockSpec(memory_space=pltpu.VMEM)] * len(pieces)
        + [anywhere] * len(filled),
        out_specs=anywhere,
        scratch_shapes=[pltpu.SemaphoreType.DMA((len(pieces),))],
        input_output_aliases={1 + len(pieces): 0} if filled else {},
        compiler_params=pltpu.CompilerParams(vmem_limit_bytes=4 * MIB),
        name="assemble",
    )(place, *pieces, *filled)


def paired(shard, x):
    length = lax.axis_size("head")
    return lax.ppermute(shard, "head", [(i, i ^ x) for i in range(length)])


def swapped(shard):
    length = lax.axis_size("ctx")
    return lax.ppermute(shard, "ctx", [(i, i ^ 1) for i in range(length)])


def crossed(shard, stage):
    length = lax.axis_size("ctx")
    bits = (length // CORES).bit_length() - 1
    bit = [stage, bits - 1 - stage]
    return lax.ppermute(
        shard, "ctx", [(i, i ^ (CORES << bit[i % CORES])) for i in range(length)]
    )


def later(shard, by):
    length = lax.axis_size("ctx")
    return lax.ppermute(shard, "ctx", [(i, i + by) for i in range(length - by)])


def body(queries, key_rows, value_rows, lengths, out_weight):
    rows = queries.shape[0]
    heads = queries.shape[1] // HD
    depth, width = out_weight.shape
    ctx, planes = lax.axis_size("ctx"), lax.axis_size("head")
    chips = ctx // CORES
    ctx_index, head_index = lax.axis_index("ctx"), lax.axis_index("head")
    chip, core = ctx_index // CORES, ctx_index % CORES
    share = depth // chips
    cols = width // (planes * CORES)
    place = jnp.stack([head_index, chip, core]).astype(jnp.int32)
    others = plane_order(planes)[1:]

    def share_of(x):
        column = ((head_index ^ x) * CORES + core) * cols
        return lax.dynamic_slice(out_weight, (chip * share, column), (share, cols))

    fetched = {x: paired(share_of(x), x) for x in others if x in (1, planes - 1)}
    own = [key_rows, value_rows]
    if key_rows.shape[1] > HD:
        column = head_index * heads // GROUP * HD
        own = [lax.dynamic_slice_in_dim(part, column, HD, 1) for part in own]
    own = jnp.concatenate(own)
    pieces = [later(own, d) for d in range(SPAN, 0, -1)] + [own]
    for x in others:
        if x not in fetched:
            fetched[x] = paired(tie(share_of(x), (fetched[planes - 1], pieces[1:-1])), x)
    groups = [[x for x in others if x in (1, planes - 1)]]
    groups.append([x for x in others if x not in groups[0]])
    plane_stages, chip_stages = planes.bit_length() - 1, chips.bit_length() - 1
    first = jnp.stack(tie([fetched[x] for x in groups[0]], pieces[1:-1]))[None]
    first = jnp.concatenate([first, crossed(first, 0)])
    rest = crossed(first, 1)
    attended = [attention(queries, pieces, lengths, ctx_index * rows)[None]]
    own_weight = lax.dynamic_slice_in_dim(
        tie(out_weight, attended), head_index * CORES * cols, CORES * cols, 1
    )

    second = jnp.stack(tie([fetched[x] for x in groups[1]], (attended, first)))[None]
    early, latest = [], attended
    for stage in range(max(plane_stages, chip_stages)):
        ahead, new, more = [], [], []
        if stage < plane_stages:
            new = [paired(jnp.concatenate(latest), (planes - 1) >> stage)]
        if stage + 1 < plane_stages:
            ahead = [paired(jnp.concatenate(attended), (planes - 1) >> (stage + 1))]
        if stage < chip_stages:
            more = [crossed(second, stage)]
        ahead, new, more, own_weight = lax.optimization_barrier((ahead, new, more, own_weight))
        latest = early + new
        attended, early = attended + latest, ahead
        second = jnp.concatenate([second] + more)
        if stage > 0 and stage + 1 < chip_stages:
            first, rest = jnp.concatenate([first, rest]), None
            rest = crossed(first, stage + 1)
    weights = [part.reshape(-1, cols) for part in (first, rest, second)]
    layout = [(k, x) for k in range(chips) for x in groups[0]]
    layout += [(k, x) for k in range(chips) for x in groups[1]]

    result = project(attended, own_weight, weights, layout, 0, place, chips)
    moved = [result[0]] + [paired(part, x) for part, x in zip(result[1:], others)]
    weights = [swapped(part) for part in weights]
    out = assemble(moved, 0, width, place)
    result = project(attended, own_weight, weights, layout, 1, place, chips)
    moved = [result[0]] + [paired(part, x) for part, x in zip(result[1:], others)]
    return assemble(moved, 1, width, place, out)


def solution(mesh):
    placed = (P("ctx", "head"), P("ctx", None), P("ctx", None), P(), P("head", None))
    return jax.shard_map(
        body, mesh=mesh, in_specs=placed, out_specs=P(("ctx", "head"), None), check_vma=False
    )
```

```python
import functools
import math

import jax
import jax.numpy as jnp
from jax import lax
from jax.experimental import pallas as pl
from jax.experimental.pallas import tpu as pltpu
from jax.sharding import PartitionSpec as P

HD = 128
GROUP = 16
SPAN = 4
CORES = 2
MIB = 1024 * 1024

big_negative = -1e30
log2_scale = math.log2(math.e) / math.sqrt(HD)


def attention_kernel(place_ref, query_hbm, *refs):
    piece_refs, (out_ref, query_ref, sem) = refs[:-3], refs[-3:]
    query_copy = pltpu.make_async_copy(query_hbm, query_ref, sem)
    query_copy.start()
    rows = query_ref.shape[0]
    heads = query_ref.shape[1] // HD
    window = rows * len(piece_refs)
    first = place_ref[0]
    query_pos = first + lax.broadcasted_iota(jnp.int32, (rows, 1), 0)

    def step(d, carry):
        end, start = carry
        end = end + place_ref[1 + d]
        return end, jnp.where(query_pos >= end, end, start)

    _, doc_start = lax.fori_loop(
        0, place_ref.shape[0] - 1, step, (jnp.int32(0), jnp.zeros((rows, 1), jnp.int32))
    )
    key_pos = first - (window - rows) + lax.broadcasted_iota(jnp.int32, (rows, window), 1)
    allowed = (key_pos >= doc_start) & (key_pos <= query_pos)
    keys = jnp.concatenate([ref[:rows] for ref in piece_refs], axis=0)
    values = jnp.concatenate([ref[rows:] for ref in piece_refs], axis=0)
    query_copy.wait()
    for head in range(heads):
        query = query_ref[:, head * HD : (head + 1) * HD]
        scores = lax.dot_general(
            query, keys, (((1,), (1,)), ((), ())), preferred_element_type=jnp.float32
        )
        scores = jnp.where(allowed, scores * log2_scale, big_negative)
        top = jnp.max(scores, axis=1, keepdims=True)
        expo = jnp.exp2(scores - top)
        total = jnp.sum(expo, axis=1, keepdims=True)
        summed = jnp.dot(expo.astype(jnp.bfloat16), values, preferred_element_type=jnp.float32)
        out_ref[:, head * HD : (head + 1) * HD] = (summed / total).astype(jnp.bfloat16)


def attention(queries, pieces, lengths, first_row):
    vmem = pl.BlockSpec(memory_space=pltpu.VMEM)
    return pl.pallas_call(
        attention_kernel,
        out_shape=jax.ShapeDtypeStruct(queries.shape, jnp.bfloat16),
        in_specs=[
            pl.BlockSpec(memory_space=pltpu.SMEM),
            pl.BlockSpec(memory_space=pltpu.HBM),
        ]
        + [vmem] * len(pieces),
        out_specs=vmem,
        scratch_shapes=[pltpu.VMEM(queries.shape, queries.dtype), pltpu.SemaphoreType.DMA],
        compiler_params=pltpu.CompilerParams(vmem_limit_bytes=24 * MIB),
        cost_estimate=pl.CostEstimate(flops=0, bytes_accessed=0, transcendentals=0),
        name="attention",
    )(jnp.concatenate([first_row[None], lengths]), queries, *pieces)


def tie(values, after):
    return lax.optimization_barrier((values, after))[0]


def chip_order(chips, core):
    bits = chips.bit_length() - 1
    return [
        sum(((k >> t) & 1) << (t if core == 0 else bits - 1 - t) for t in range(bits))
        for k in range(chips)
    ]


def plane_order(planes):
    order, mask = [0], planes - 1
    while mask:
        order += [x ^ mask for x in order]
        mask >>= 1
    return order


def project(attended, own_weight, weights, layout, half, place, chips):
    order = plane_order(sum(part.shape[0] for part in attended))
    planes = len(order)
    _, rows, depth = attended[0].shape
    cols = own_weight.shape[1] // CORES
    share = depth // chips
    rows_out = rows // planes
    block = min(cols, 1024)
    size = (planes - 1) * depth
    aligned = share % HD == 0
    chip_orders = [chip_order(chips, core) for core in range(CORES)]
    operands = list(attended)
    if not aligned:
        others = jnp.concatenate(attended).reshape(planes, rows, chips, share)
        chip_index = place[1] ^ jnp.asarray(chip_orders)[(place[2] + half) % CORES]
        chip_index = chip_index[jnp.asarray([k for k, _ in layout])]
        plane_index = jnp.asarray([order.index(x) for _, x in layout])
        others = others.transpose(0, 2, 1, 3)[plane_index, chip_index]
        operands = [attended[0][0], others.transpose(1, 0, 2).reshape(rows, size)]

    def kernel(place_ref, *refs):
        attended_refs, refs = refs[: len(operands)], refs[len(operands) :]
        own_ref, refs = refs[0], refs[1:]
        weight_refs, refs = refs[: len(weights)], refs[len(weights) :]
        out_refs, (flat_ref, wide_ref) = refs[:planes], refs[planes:]
        head, chip = place_ref[0], place_ref[1]
        core = (place_ref[2] + half) % CORES

        blocks = [(ref, i) for ref in attended_refs for i in range(ref.shape[0])] * aligned
        for d, dest in enumerate(order):
            source = pl.ds(pl.multiple_of((head ^ dest) * rows_out, rows_out), rows_out)
            to = slice(d * rows_out, (d + 1) * rows_out)
            if not aligned:
                flat_ref[to, :] = attended_refs[0][source, :]
                wide_ref[to, :] = attended_refs[1][source, :]
                continue
            flat_ref[to, :] = attended_refs[0][0, source, :]
            for at, (k, x) in enumerate(layout):
                low, high = (chip_orders[c][k] for c in range(CORES))
                index = chip ^ (low + core * (high - low))
                column = pl.ds(pl.multiple_of(index * share, share), share)
                ref, i = blocks[order.index(x)]
                wide_ref[to, at * share : (at + 1) * share] = ref[i, source, column]

        for j in range(cols // block):
            columns = slice(j * block, (j + 1) * block)
            own = own_ref[:, pl.ds(pl.multiple_of(core * cols + j * block, HD), block)]
            acc = jnp.dot(flat_ref[...], own, preferred_element_type=jnp.float32)
            at = 0
            for ref in weight_refs:
                acc += jnp.dot(
                    wide_ref[:, at : at + ref.shape[0]],
                    ref[:, columns],
                    preferred_element_type=jnp.float32,
                )
                at += ref.shape[0]
            acc = acc.astype(jnp.bfloat16)
            for d, out_ref in enumerate(out_refs):
                out_ref[:, columns] = acc[d * rows_out : (d + 1) * rows_out]

    vmem = pl.BlockSpec(memory_space=pltpu.VMEM)
    return pl.pallas_call(
        kernel,
        out_shape=[jax.ShapeDtypeStruct((rows_out, cols), jnp.bfloat16)] * planes,
        in_specs=[pl.BlockSpec(memory_space=pltpu.SMEM)]
        + [vmem] * (len(operands) + 1 + len(weights)),
        out_specs=[vmem] * planes,
        scratch_shapes=[
            pltpu.VMEM((rows, depth), jnp.bfloat16),
            pltpu.VMEM((rows, size), jnp.bfloat16),
        ],
        compiler_params=pltpu.CompilerParams(vmem_limit_bytes=20 * MIB),
        cost_estimate=pl.CostEstimate(
            flops=2 * rows * planes * depth * cols,
            bytes_accessed=2 * (planes * depth * (rows + cols) + rows * cols),
            transcendentals=0,
        ),
        name="project",
    )(place, *operands, own_weight, *weights)


def assemble(pieces, half, width, place, out=None):
    order = plane_order(len(pieces))
    rows, cols = pieces[0].shape
    filled = [] if out is None else [out]

    def kernel(place_ref, *refs):
        out_ref, sem = refs[-2:]
        copies = []
        for k, x in enumerate(order):
            at = ((place_ref[0] ^ x) * CORES + (place_ref[2] + half) % CORES) * cols
            copies.append(
                pltpu.make_async_copy(
                    refs[k], out_ref.at[:, pl.ds(pl.multiple_of(at, HD), cols)], sem.at[k]
                )
            )
        for copy in copies:
            copy.start()
        for copy in copies:
            copy.wait()

    anywhere = pl.BlockSpec(memory_space=pl.ANY)
    return pl.pallas_call(
        kernel,
        out_shape=jax.ShapeDtypeStruct((rows, width), jnp.bfloat16),
        in_specs=[pl.BlockSpec(memory_space=pltpu.SMEM)]
        + [pl.BlockSpec(memory_space=pltpu.VMEM)] * len(pieces)
        + [anywhere] * len(filled),
        out_specs=anywhere,
        scratch_shapes=[pltpu.SemaphoreType.DMA((len(pieces),))],
        input_output_aliases={1 + len(pieces): 0} if filled else {},
        compiler_params=pltpu.CompilerParams(vmem_limit_bytes=4 * MIB),
        name="assemble",
    )(place, *pieces, *filled)


def paired(shard, x):
    length = lax.axis_size("head")
    return lax.ppermute(shard, "head", [(i, i ^ x) for i in range(length)])


def swapped(shard):
    length = lax.axis_size("ctx")
    return lax.ppermute(shard, "ctx", [(i, i ^ 1) for i in range(length)])


def crossed(shard, stage):
    length = lax.axis_size("ctx")
    bits = (length // CORES).bit_length() - 1
    bit = [stage, bits - 1 - stage]
    return lax.ppermute(
        shard, "ctx", [(i, i ^ (CORES << bit[i % CORES])) for i in range(length)]
    )


def later(shard, by):
    length = lax.axis_size("ctx")
    return lax.ppermute(shard, "ctx", [(i, i + by) for i in range(length - by)])


def body(queries, key_rows, value_rows, lengths, out_weight):
    rows = queries.shape[0]
    heads = queries.shape[1] // HD
    depth, width = out_weight.shape
    ctx, planes = lax.axis_size("ctx"), lax.axis_size("head")
    chips = ctx // CORES
    ctx_index, head_index = lax.axis_index("ctx"), lax.axis_index("head")
    chip, core = ctx_index // CORES, ctx_index % CORES
    share = depth // chips
    cols = width // (planes * CORES)
    place = jnp.stack([head_index, chip, core]).astype(jnp.int32)
    others = plane_order(planes)[1:]

    def share_of(x):
        column = ((head_index ^ x) * CORES + core) * cols
        return lax.dynamic_slice(out_weight, (chip * share, column), (share, cols))

    fetched = {x: paired(share_of(x), x) for x in others if x in (1, planes - 1)}
    own = [key_rows, value_rows]
    if key_rows.shape[1] > HD:
        column = head_index * heads // GROUP * HD
        own = [lax.dynamic_slice_in_dim(part, column, HD, 1) for part in own]
    own = jnp.concatenate(own)
    pieces = [later(own, d) for d in range(SPAN, 0, -1)] + [own]
    for x in others:
        if x not in fetched:
            fetched[x] = paired(tie(share_of(x), (fetched[planes - 1], pieces[1:-1])), x)
    groups = [[x for x in others if x in (1, planes - 1)]]
    groups.append([x for x in others if x not in groups[0]])
    plane_stages, chip_stages = planes.bit_length() - 1, chips.bit_length() - 1
    first = jnp.stack(tie([fetched[x] for x in groups[0]], pieces[1:-1]))[None]
    first = jnp.concatenate([first, crossed(first, 0)])
    rest = crossed(first, 1)
    attended = [attention(queries, pieces, lengths, ctx_index * rows)[None]]
    own_weight = lax.dynamic_slice_in_dim(
        tie(out_weight, attended), head_index * CORES * cols, CORES * cols, 1
    )

    second = jnp.stack(tie([fetched[x] for x in groups[1]], (attended, first)))[None]
    early, latest = [], attended
    for stage in range(max(plane_stages, chip_stages)):
        ahead, new, more = [], [], []
        if stage < plane_stages:
            new = [paired(jnp.concatenate(latest), (planes - 1) >> stage)]
        if stage + 1 < plane_stages:
            ahead = [paired(jnp.concatenate(attended), (planes - 1) >> (stage + 1))]
        if stage < chip_stages:
            more = [crossed(second, stage)]
        ahead, new, more, own_weight = lax.optimization_barrier((ahead, new, more, own_weight))
        latest = early + new
        attended, early = attended + latest, ahead
        second = jnp.concatenate([second] + more)
        if stage > 0 and stage + 1 < chip_stages:
            first, rest = jnp.concatenate([first, rest]), None
            rest = crossed(first, stage + 1)
    weights = [part.reshape(-1, cols) for part in (first, rest, second)]
    layout = [(k, x) for k in range(chips) for x in groups[0]]
    layout += [(k, x) for k in range(chips) for x in groups[1]]

    result = project(attended, own_weight, weights, layout, 0, place, chips)
    moved = [result[0]] + [paired(part, x) for part, x in zip(result[1:], others)]
    weights = [swapped(part) for part in weights]
    out = assemble(moved, 0, width, place)
    result = project(attended, own_weight, weights, layout, 1, place, chips)
    moved = [result[0]] + [paired(part, x) for part, x in zip(result[1:], others)]
    return assemble(moved, 1, width, place, out)


def solution(mesh):
    placed = (P("ctx", "head"), P("ctx", None), P("ctx", None), P(), P("head", None))
    return jax.shard_map(
        body, mesh=mesh, in_specs=placed, out_specs=P(("ctx", "head"), None), check_vma=False
    )
```
